32 devices in a mesh: dp: 8 (over z, y), expert: 4 (over x, core).
Axes of the slice: x: 2, y: 2, z: 4, core: 2. Of those that a mesh axis runs over, the one named last changes fastest.
Arguments:
- tokens: bfloat16 [4096, 2048], P(('dp', 'expert')), may hold values from -6 to 6
- routes: int32 [4096, 2], P(('dp', 'expert')), may hold values from 0 to 15, all different within a row; in each aligned block of 128 rows (0 to 127, 128 to 255, ...) at most 32 rows name the same one
- gate_codes: int32 [4096, 2], P(('dp', 'expert')), may hold values from 1 to 1024
- w_gate: bfloat16 [32, 2048, 384], P(('dp', 'expert')), may hold values from -0.125 to 0.125
- w_up: bfloat16 [32, 2048, 384], P(('dp', 'expert')), may hold values from -0.125 to 0.125
- w_down: bfloat16 [32, 384, 2048], P(('dp', 'expert')), may hold values from -0.21875 to 0.21875
- cot: bfloat16 [4096, 2048], P(('dp', 'expert')), may hold values from -6 to 6
Outputs:
- mixed: bfloat16 [4096, 2048], P(('dp', 'expert'))
- d_tokens: bfloat16 [4096, 2048], P(('dp', 'expert'))
- d_gate: bfloat16 [32, 2048, 384], P(('dp', 'expert'))
- d_up: bfloat16 [32, 2048, 384], P(('dp', 'expert'))
- d_down: bfloat16 [32, 384, 2048], P(('dp', 'expert'))
The draws below stay inside these ranges and needn't reach their ends.
Inputs may be any that keep to these rules, and one draw needn't show every extreme that they name: `routes`: each row names 2 different experts; among the 128 rows of one device no expert is named more than 32 times, a bound that some block reaches. `gate_codes`: the gate weight is the value divided by 1024.
All inputs are finite; a program needn't handle non-finite values.
Results may differ from the reference program's by a relative error of at most 0.012.
Values may be sent and summed in bfloat16 or wider, within the bound.
A program may use at most 128 MiB of HBM per device.

```python
import math
import jax
import jax.numpy as jnp
import numpy as np
from jax import lax

D = 2048
F = 768
TOP = 2
TOK_DEV = 128
FH = 384
EXPERTS = 16
SUBS = 32
MOST = 32
TOKENS = 4096
N_DP = 8
N_EXPERT = 4


def plant(values, stream_key, low, high):
    shape = values.shape
    spot = [jax.random.randint(jax.random.fold_in(stream_key, axis), (), 0, shape[axis]) for axis in range(len(shape))]
    values = values.at[tuple(spot)].set(low)
    longest = shape.index(max(shape))
    spot[longest] = (spot[longest] + 1) % shape[longest]
    return values.at[tuple(spot)].set(high)


def levels(stream_key, extent, shards, low, high):
    factor_of, own = 1.0, jax.random.fold_in(stream_key, 6)
    for dim, parts in shards:
        steps = jnp.exp(jax.random.uniform(jax.random.fold_in(own, dim), (parts,), jnp.float32, low / len(shards), high / len(shards)))
        factor_of = factor_of * jnp.repeat(steps, extent[dim] // parts).reshape([-1 if axis == dim else 1 for axis in range(len(extent))])
    return factor_of


def assign_block(key, own, number, rows, amount, top, reach, slope):
    order = jax.random.permutation(key, amount)
    packed, ordinary = portions_of(amount, rows * top, reach, slope, True), portions_of(amount, rows * top, reach, slope, False)
    places = jnp.arange(amount)

    def named(sizes, turn):
        used = int((sizes > 0).sum())
        fixed = max(1, used // 4)
        moved = fixed + (places - fixed + turn * (used - fixed)) % max(1, amount - fixed)
        return jnp.zeros((amount,), jnp.int32).at[order[jnp.where(places < fixed, places, moved)]].set(jnp.asarray(sizes, jnp.int32))

    sizes = jnp.where(number % 4 == 0, named(packed, number // 4), named(ordinary, number - number // 4 - 1))
    mixed = jax.random.permutation(jax.random.fold_in(own, 3), amount)
    donor, receiver = mixed[0:amount // 2 * 2:2], mixed[1:amount // 2 * 2:2]
    slack = jnp.minimum(sizes[donor] - 1, reach - sizes[receiver]) // 2
    slack = jnp.where((donor == order[0]) | (receiver == order[0]) | (sizes[receiver] == 0), 0, jnp.maximum(slack, 0))
    moved = jax.random.randint(jax.random.fold_in(own, 4), (amount // 2,), 0, 1 << 20) % (slack + 1)
    sizes = sizes.at[donor].add(-moved).at[receiver].add(moved)
    items = jnp.searchsorted(jnp.cumsum(sizes), jnp.arange(rows * top), side="right").astype(jnp.int32)
    table = items.reshape(top, rows).T
    table = table[jax.random.permutation(jax.random.fold_in(own, 1), rows)]
    turn = jax.random.randint(jax.random.fold_in(own, 2), (rows, 1), 0, top)
    return jnp.take_along_axis(table, (jnp.arange(top)[None, :] + turn) % top, axis=1)


def portions_of(count, total, reach, slope, full):
    loads = [(1 << 20) // math.isqrt(rank ** slope) + 1 for rank in range(1, count + 1)]
    largest = reach if full else min(reach, max(-(-total // count), total * loads[0] // sum(loads)))
    least = 1 if total - largest >= count - 1 else 0
    holding, spare = [largest] + [least] * (count - 1), total - largest - least * (count - 1)
    while spare > 0:
        candidates = [i for i in range(1, count) if holding[i] < largest] or [i for i in range(1, count) if holding[i] < reach]
        whole, budget = sum([loads[i] for i in candidates]), spare
        for i in candidates:
            more = min(reach - holding[i], max(1, budget * loads[i] // whole), spare)
            holding[i] = holding[i] + more
            spare = spare - more
    return np.array(holding)


def normal_values(own_key, shape, spread, reach, split=(), kind=jnp.bfloat16):
    values = spread * jax.random.normal(own_key, shape, jnp.float32)
    if split:
        values = values * levels(own_key, shape, split, -0.22, 0.18)
    return jnp.clip(values, -reach, reach).astype(kind)


def setup_inputs(seed: int = 0) -> dict:
    key_of = jax.random.split(jax.random.key(seed), 8)
    tokens = normal_values(key_of[0], (TOKENS, D), 1.0, 6.0, ((0, 32),))
    routes_keys = jax.random.split(jax.random.fold_in(key_of[1], 1), TOKENS // TOK_DEV)
    routes_turns = jax.random.permutation(jax.random.fold_in(key_of[1], 3), TOKENS // TOK_DEV)
    routes = jax.vmap(lambda own, number: assign_block(jax.random.fold_in(key_of[1], 2), own, number, TOK_DEV, EXPERTS, TOP, MOST, 2))(routes_keys, routes_turns).reshape((TOKENS, TOP))
    gate_codes = plant(jax.random.randint(key_of[2], (TOKENS, TOP), 1, 1025), jax.random.fold_in(key_of[2], 1), 1, 1024).astype(jnp.int32)
    w_gate = normal_values(key_of[3], (SUBS, D, FH), D ** -0.5, 0.125, ((0, 32),))
    w_up = normal_values(key_of[4], (SUBS, D, FH), D ** -0.5, 0.125, ((0, 32),))
    w_down = normal_values(key_of[5], (SUBS, FH, D), F ** -0.5, 0.21875, ((0, 32),))
    cot = normal_values(key_of[6], (TOKENS, D), 1.0, 6.0, ((0, 32),))
    return dict(tokens=tokens, routes=routes, gate_codes=gate_codes, w_gate=w_gate, w_up=w_up, w_down=w_down, cot=cot)


def rounded(value):
    return lax.optimization_barrier(value.astype(jnp.bfloat16)).astype(jnp.float32)


def reference(tokens, routes, gate_codes, w_gate, w_up, w_down, cot):
    tok_all, top = routes.shape
    width = tokens.shape[1]
    half = w_gate.shape[2]
    experts = w_gate.shape[0] // 2
    capacity = MOST * N_DP * N_EXPERT
    pairs = tok_all * top
    expert_ids = routes.reshape(pairs)
    onehot = (expert_ids[:, None] == jnp.arange(experts, dtype=jnp.int32)[None, :]).astype(jnp.int32)
    before = jnp.cumsum(onehot, axis=0) - onehot
    position = jnp.sum(before * onehot, axis=1).astype(jnp.int32)
    table = jnp.full((experts, capacity), pairs, jnp.int32).at[expert_ids, position].set(jnp.arange(pairs, dtype=jnp.int32))
    gates = gate_codes.reshape(pairs).astype(jnp.float32) / 1024.0
    gates_pad = jnp.concatenate([gates, jnp.zeros((1,), jnp.float32)])
    tok_pad = jnp.concatenate([tokens, jnp.zeros((1, width), jnp.bfloat16)], axis=0)
    cot_pad = jnp.concatenate([cot, jnp.zeros((1, width), jnp.bfloat16)], axis=0)
    wg_full = w_gate.reshape(experts, 2, width, half).transpose(0, 2, 1, 3).reshape(experts, width, 2 * half)
    wu_full = w_up.reshape(experts, 2, width, half).transpose(0, 2, 1, 3).reshape(experts, width, 2 * half)
    wd_full = w_down.reshape(experts, 2 * half, width)

    def one_expert(carry, inputs):
        out_acc, grad_acc = carry
        slots, wg, wu, wd = inputs
        token_idx = jnp.where(slots < pairs, slots // top, tok_all).astype(jnp.int32)
        weight = gates_pad[slots]
        xrows = tok_pad[token_idx]
        act = jnp.dot(xrows, wg, preferred_element_type=jnp.float32)
        upv = jnp.dot(xrows, wu, preferred_element_type=jnp.float32)
        sig = jax.nn.sigmoid(act)
        silu = act * sig
        hidden = (silu * upv).astype(jnp.bfloat16)
        out_lo = rounded(jnp.dot(hidden[:, :half], wd[:half], preferred_element_type=jnp.float32))
        out_hi = rounded(jnp.dot(hidden[:, half:], wd[half:], preferred_element_type=jnp.float32))
        qrows = (weight[:, None] * cot_pad[token_idx].astype(jnp.float32)).astype(jnp.bfloat16)
        dhid = jnp.dot(qrows, wd.T, preferred_element_type=jnp.float32)
        dact = (dhid * upv * sig * (1.0 + act * (1.0 - sig))).astype(jnp.bfloat16)
        dupv = (dhid * silu).astype(jnp.bfloat16)
        grad_lo = rounded(jnp.dot(dact[:, :half], wg[:, :half].T, preferred_element_type=jnp.float32) + jnp.dot(dupv[:, :half], wu[:, :half].T, preferred_element_type=jnp.float32))
        grad_hi = rounded(jnp.dot(dact[:, half:], wg[:, half:].T, preferred_element_type=jnp.float32) + jnp.dot(dupv[:, half:], wu[:, half:].T, preferred_element_type=jnp.float32))
        grad_g = jnp.dot(xrows.T, dact, preferred_element_type=jnp.float32).astype(jnp.bfloat16)
        grad_u = jnp.dot(xrows.T, dupv, preferred_element_type=jnp.float32).astype(jnp.bfloat16)
        grad_d = jnp.dot(hidden.T, qrows, preferred_element_type=jnp.float32).astype(jnp.bfloat16)
        out_acc = out_acc.at[token_idx].add(weight[:, None] * (out_lo + out_hi))
        grad_acc = grad_acc.at[token_idx].add(grad_lo + grad_hi)
        return (out_acc, grad_acc), (grad_g, grad_u, grad_d)

    start = (jnp.zeros((tok_all + 1, width), jnp.float32), jnp.zeros((tok_all + 1, width), jnp.float32))
    (out_acc, grad_acc), (grad_g, grad_u, grad_d) = lax.scan(one_expert, start, (table, wg_full, wu_full, wd_full))
    mixed = out_acc[:tok_all].astype(jnp.bfloat16)
    d_tokens = grad_acc[:tok_all].astype(jnp.bfloat16)
    d_gate = grad_g.reshape(experts, width, 2, half).transpose(0, 2, 1, 3).reshape(2 * experts, width, half)
    d_up = grad_u.reshape(experts, width, 2, half).transpose(0, 2, 1, 3).reshape(2 * experts, width, half)
    d_down = grad_d.reshape(2 * experts, half, width)
    return (mixed, d_tokens, d_gate, d_up, d_down)
```

```python
import jax
import jax.numpy as jnp
from jax import lax
from jax.sharding import PartitionSpec as P

AXES = ("dp", "expert")
BF = jnp.bfloat16
F32 = jnp.float32


def dot(a, b):
    return jnp.dot(a, b, preferred_element_type=F32)


def dot_nt(a, b):
    return lax.dot_general(a, b, (((1,), (1,)), ((), ())), preferred_element_type=F32)


def dot_tn(a, b):
    return lax.dot_general(a, b, (((0,), (0,)), ((), ())), preferred_element_type=F32)


def local(tokens, routes, gate_codes, w_gate, w_up, w_down, cot):
    tok_rows, top = routes.shape
    width = tokens.shape[1]
    n_group = lax.axis_size("expert")
    devices = lax.axis_size("dp") * n_group
    experts = devices // 2
    most = max(2, 2 * tok_rows * top // experts)
    slots = experts * most
    same_core = [list(range(core, devices, 2)) for core in range(2)]
    sibling = [(i, i ^ 1) for i in range(n_group)]

    def exchange(rows):
        blocks = rows.reshape(experts, most, width)
        blocks = lax.all_to_all(
            blocks, AXES, split_axis=0, concat_axis=0, axis_index_groups=same_core, tiled=True
        )
        return blocks.reshape(slots, width)

    def swap(rows):
        return lax.ppermute(rows, "expert", sibling)

    expert_ids = routes.reshape(tok_rows * top)
    onehot = (expert_ids[:, None] == jnp.arange(experts, dtype=jnp.int32)[None, :]).astype(
        jnp.int32
    )
    before = jnp.cumsum(onehot, axis=0) - onehot
    position = jnp.sum(before * onehot, axis=1)
    target = (expert_ids * most + position).reshape(tok_rows, top)
    slot_ids = jnp.arange(slots, dtype=jnp.int32)
    place = jnp.zeros((slots, tok_rows), BF)
    code_hi = jnp.zeros((tok_rows, slots), BF)
    code_lo = jnp.zeros((tok_rows, slots), BF)
    gate_slot = jnp.zeros((slots, 1), F32)
    low = gate_codes % 8
    for k in range(top):
        hit = slot_ids[:, None] == target[None, :, k]
        place = place + hit.astype(BF)
        gate_slot = gate_slot + jnp.sum(
            jnp.where(hit, gate_codes[None, :, k].astype(F32), 0.0), axis=1, keepdims=True
        )
        hit_t = target[:, k, None] == slot_ids[None, :]
        code_hi = code_hi + jnp.where(hit_t, (gate_codes - low)[:, k, None], 0).astype(BF)
        code_lo = code_lo + jnp.where(hit_t, low[:, k, None], 0).astype(BF)
    gate_slot = gate_slot / 1024.0

    wg, wu, wd = w_gate[0], w_up[0], w_down[0]
    xmine = exchange(dot(place, tokens).astype(BF))
    qmine = exchange((gate_slot * dot(place, cot)).astype(BF))

    xrows = jnp.concatenate([xmine, swap(xmine)], axis=0)
    act = dot(xrows, wg)
    upv = dot(xrows, wu)
    sig = jax.nn.sigmoid(act)
    silu = act * sig
    hidden = (silu * upv).astype(BF)

    def give_back(rows):
        other = swap(rows[slots:])
        return exchange((rows[:slots].astype(F32) + other.astype(F32)).astype(BF))

    oback = give_back(dot(hidden, wd).astype(BF))

    qrows = jnp.concatenate([qmine, swap(qmine)], axis=0)
    dhid = dot_nt(qrows, wd)
    dact = (dhid * upv * sig * (1.0 + act * (1.0 - sig))).astype(BF)
    dupv = (dhid * silu).astype(BF)
    pback = give_back((dot_nt(dact, wg) + dot_nt(dupv, wu)).astype(BF))

    grad_g = dot_tn(xrows, dact).astype(BF)
    grad_u = dot_tn(xrows, dupv).astype(BF)
    grad_d = dot_tn(hidden, qrows).astype(BF)

    mixed = ((dot(code_hi, oback) + dot(code_lo, oback)) / 1024.0).astype(BF)
    d_tokens = dot_tn(place, pback).astype(BF)
    return (mixed, d_tokens, grad_g[None], grad_u[None], grad_d[None])


def solution(mesh):
    rows = P(AXES, None)
    stack = P(AXES, None, None)
    return jax.shard_map(
        local,
        mesh=mesh,
        in_specs=(rows, rows, rows, stack, stack, stack, rows),
        out_specs=(rows, rows, stack, stack, stack),
        check_vma=False,
    )
```
